32 devices in a mesh: dp: 8 (over z, y), mp: 4 (over x, core).
Axes of the slice: x: 2, y: 2, z: 4, core: 2. Of those that a mesh axis runs over, the one named last changes fastest.
Arguments:
- stream_map: int32 [8], replicated, may hold values from 0 to 7, each once
- lengths: int32 [8], P('dp'), may hold values from 1 to 256, 1280 in all
- features: bfloat16 [8, 256, 2048], P('dp', None, 'mp'), may hold values from -6 to 6
- query_rows: bfloat16 [8, 256, 2048], P('dp', None, 'mp'), may hold values from -6 to 6
- key_rows: bfloat16 [8, 256, 2048], P('dp', None, 'mp'), may hold values from -6 to 6
- log_forget: float32 [8, 256, 4], P('dp', None, 'mp'), may hold values from -1 to 0, as said below
- in_gate: float32 [8, 256, 4], P('dp', None, 'mp'), may hold values from -2 to 2
- value_weight: bfloat16 [2048, 2048], P('dp', 'mp'), may hold values from -0.125 to 0.125
- state: float32 [8, 4, 512, 512], P('dp', 'mp'), may hold values from -0.5 to 0.5
- norm_state: float32 [8, 4, 512], P('dp', 'mp'), may hold values from -0.8 to 0.8
- cotangent: bfloat16 [8, 256, 2048], P('dp', None, 'mp'), may hold values from -6 to 6
Outputs:
- hidden: bfloat16 [8, 256, 2048], P('dp', None, 'mp')
- new_state: float32 [8, 4, 512, 512], P('dp', 'mp')
- new_norm: float32 [8, 4, 512], P('dp', 'mp')
- weight_grad: float32 [2048, 2048], P('dp', 'mp')
The draws below stay inside these ranges and needn't reach their ends.
Inputs may be any that keep to these rules, and one draw needn't show every extreme that they name: stream_map is a permutation of the 8 slots. `lengths`: the largest length is exactly 256. `log_forget`: all entries negative.
All inputs are finite; a program needn't handle non-finite values. No bound on the sum of `lengths` on one device may be relied on, other than what follows from the above.
Results may differ from the reference program's by a relative error of at most 0.0065.
Values may be sent and summed in bfloat16 or wider, within the bound.
A program may use at most 64 MiB of HBM per device.

```python
import math
import jax
import jax.numpy as jnp
import numpy as np
from jax import lax

DIN = 2048
HEAD_COUNT = 4
DH = 512
TOKEN_SLOTS = 256
STREAM_COUNT = 8


def draw_log_forget(key, part):
    random_subkeys = jax.random.split(key, 5)
    low_rate = 0.2 / TOKEN_SLOTS
    high_rate = 1.0 / 30.0
    per_head_rate = jnp.exp(jax.random.uniform(random_subkeys[0], (1, 1, HEAD_COUNT), jnp.float32, math.log(low_rate), math.log(high_rate)))
    stream_multiplier = jnp.exp(jax.random.uniform(random_subkeys[1], (STREAM_COUNT, 1, 1), jnp.float32, math.log(0.5), math.log(2.0)))
    random_noise = jax.random.uniform(random_subkeys[2], (STREAM_COUNT, TOKEN_SLOTS, HEAD_COUNT), jnp.float32, 0.5, 1.5)
    spike_positions = jax.random.randint(random_subkeys[3], (STREAM_COUNT, 2, HEAD_COUNT), 0, TOKEN_SLOTS)
    loss_values = jnp.log(jax.random.uniform(random_subkeys[4], (STREAM_COUNT, 2, HEAD_COUNT), jnp.float32, 0.6, 0.8))
    spike_flags = (spike_positions[..., None] == jnp.arange(TOKEN_SLOTS)[None, None, None, :]).astype(jnp.float32)
    spike_events = jnp.einsum('dxea,dxe->dae', spike_flags, loss_values)
    return jnp.maximum(-per_head_rate * stream_multiplier * random_noise + spike_events, -1.0)


def strengthened(drawn, rng, source, target, blocks, factor):
    owner, partner = [(jnp.arange(drawn.shape[dim]) // (drawn.shape[dim] // blocks)).reshape([-1 if axis == dim else 1 for axis in range(drawn.ndim)]) for dim in (source, target)]
    chosen = jax.random.permutation(rng, blocks)[partner]
    strong = (owner == chosen) | (owner == (partner + blocks // 2) % blocks)
    return jnp.where(strong, factor * drawn, drawn)


def levels(own_key, shape, cuts, smallest, top_value):
    level, own = 1.0, jax.random.fold_in(own_key, 6)
    for dim, blocks in cuts:
        draws = jnp.exp(jax.random.uniform(jax.random.fold_in(own, dim), (blocks,), jnp.float32, smallest / len(cuts), top_value / len(cuts)))
        level = level * jnp.repeat(draws, shape[dim] // blocks).reshape([-1 if axis == dim else 1 for axis in range(len(shape))])
    return level


def length_profile(number_of, total, most, skew):
    loads = [(1 << 20) // math.isqrt(grade ** skew) + 1 for grade in range(2, number_of + 1)]
    rest, holding = total - most - (number_of - 1), [1] * (number_of - 1)
    while rest > 0:
        movable = [i for i in range(number_of - 1) if holding[i] < most]
        whole, budget = sum([loads[i] for i in movable]), rest
        for i in movable:
            addition = min(most - holding[i], max(1, budget * loads[i] // whole), rest)
            holding[i] = holding[i] + addition
            rest = rest - addition
    return np.array([most] + holding)


def uneven(key, count, total, reach, slope):
    if count == 2:
        one = jax.random.randint(key, (), max(1, total - reach), min(reach, total - 1) + 1)
        return jnp.stack([one, total - one])
    sizes = jnp.asarray(length_profile(count, total, reach, slope), jnp.int32)
    twos = (count - 1) // 2
    giver, receiver = sizes[1:1 + 2 * twos:2], sizes[2:2 + 2 * twos:2]
    margin = jnp.minimum(giver - 1, reach - receiver)
    passed = jax.random.randint(jax.random.fold_in(key, 1), (twos,), 0, 1 << 20) % (margin + 1)
    sizes = sizes.at[1:1 + 2 * twos:2].set(giver - passed).at[2:2 + 2 * twos:2].set(receiver + passed)
    return sizes[jax.random.permutation(jax.random.fold_in(key, 2), count)]


def bell_draw(rng, shape, scale, bound, pieces=(), kind=jnp.bfloat16):
    factor_of = levels(rng, shape, pieces, -0.22, 0.18) if pieces else 1.0
    values = jax.random.normal(rng, shape, jnp.float32) * scale * factor_of
    return jnp.minimum(jnp.maximum(values, -bound), bound).astype(kind)


def bell_draw_with(own_key, dims, deviation, bound, shards, heavy, held_as=jnp.bfloat16):
    array = deviation * jax.random.normal(own_key, dims, jnp.float32)
    if shards:
        array = array * levels(own_key, dims, shards, -0.22, 0.18)
    return jnp.clip(strengthened(array, jax.random.fold_in(own_key, 3), *heavy), -bound, bound).astype(held_as)


def setup_inputs(seed: int = 0) -> dict:
    splits = jax.random.split(jax.random.key(seed), 12)
    stream_map = jax.random.permutation(splits[0], STREAM_COUNT).astype(jnp.int32)
    lengths = uneven(splits[1], STREAM_COUNT, STREAM_COUNT * TOKEN_SLOTS * 5 // 8, TOKEN_SLOTS, 1).astype(jnp.int32)
    features = bell_draw_with(splits[2], (STREAM_COUNT, TOKEN_SLOTS, DIN), 1.0, 6.0, ((0, 8), (2, 4)), (0, 2, 8, 2.0))
    query_rows = bell_draw(splits[3], (STREAM_COUNT, TOKEN_SLOTS, HEAD_COUNT * DH), 1.0, 6.0, ((0, 8), (2, 4)))
    key_rows = bell_draw(splits[4], (STREAM_COUNT, TOKEN_SLOTS, HEAD_COUNT * DH), 1.0, 6.0, ((0, 8), (2, 4)))
    log_forget = draw_log_forget(jax.random.fold_in(splits[11], 71), 0)
    in_gate = jnp.clip(jax.random.uniform(splits[6], (STREAM_COUNT, TOKEN_SLOTS, HEAD_COUNT), jnp.float32, -2.0, 2.0) * levels(splits[6], (STREAM_COUNT, TOKEN_SLOTS, HEAD_COUNT), ((0, 8), (2, 4)), -0.4, 0.0), -2.0, 2.0)
    value_weight = bell_draw(splits[7], (DIN, HEAD_COUNT * DH), DIN ** -0.5, 0.125, ((0, 8), (1, 4)))
    state = bell_draw(splits[8], (STREAM_COUNT, HEAD_COUNT, DH, DH), (2.0 / DH ** 0.5), 0.5, ((0, 8), (1, 4)), jnp.float32)
    norm_state = bell_draw(splits[9], (STREAM_COUNT, HEAD_COUNT, DH), (3.0 / DH ** 0.5), 0.8, ((0, 8), (1, 4)), jnp.float32)
    cotangent = bell_draw(splits[10], (STREAM_COUNT, TOKEN_SLOTS, HEAD_COUNT * DH), 1.0, 6.0, ((0, 8), (2, 4)))
    return dict(stream_map=stream_map, lengths=lengths, features=features, query_rows=query_rows, key_rows=key_rows, log_forget=log_forget, in_gate=in_gate, value_weight=value_weight, state=state, norm_state=norm_state, cotangent=cotangent)


def head_pass(features, weight, queries, key_vectors, forget_logs, gate_logs, length, start_state, start_norm, cotangent):
    window = features.shape[0]
    head_width = queries.shape[1]
    values = jnp.dot(features, weight, preferred_element_type=jnp.float32).astype(jnp.bfloat16)
    position = jnp.arange(window, dtype=jnp.int32)
    live_mask = (position < length).astype(jnp.float32)
    decays = jnp.cumsum(forget_logs * live_mask)
    weights_in = jnp.exp(gate_logs) * live_mask
    causal = position[:, None] >= position[None, :]
    gap_logs = jnp.where(causal, decays[:, None] - decays[None, :], -1e30)
    mixing = jnp.exp(gap_logs) * weights_in[None, :]
    scores = lax.dot_general(queries, key_vectors, (((1,), (1,)), ((), ())), preferred_element_type=jnp.float32) * (head_width ** -0.5)
    combined = mixing * scores
    combined_low = combined.astype(jnp.bfloat16)
    carried = jnp.exp(decays)
    query_wide = queries.astype(jnp.float32)
    from_state = jnp.dot(query_wide, start_state, precision=lax.Precision.HIGHEST)
    numer = carried[:, None] * from_state + jnp.dot(combined_low, values, preferred_element_type=jnp.float32)
    inner_dot = carried * jnp.dot(query_wide, start_norm, precision=lax.Precision.HIGHEST) + jnp.sum(combined, axis=1)
    denominator = jnp.maximum(jnp.abs(inner_dot), 1.0)
    hidden = (numer / denominator[:, None] * live_mask[:, None]).astype(jnp.bfloat16)
    final_decay = decays[window - 1]
    tail_weight = jnp.exp(final_decay - decays) * weights_in * (head_width ** -0.5)
    key_scaled = (key_vectors.astype(jnp.float32) * tail_weight[:, None]).astype(jnp.bfloat16)
    new_state = jnp.exp(final_decay) * start_state + lax.dot_general(key_scaled, values, (((0,), (0,)), ((), ())), preferred_element_type=jnp.float32)
    new_norm = jnp.exp(final_decay) * start_norm + jnp.dot(tail_weight, key_vectors.astype(jnp.float32), precision=lax.Precision.HIGHEST)
    scaled = (cotangent.astype(jnp.float32) * (live_mask / denominator)[:, None]).astype(jnp.bfloat16)
    value_grad = lax.dot_general(combined_low, scaled, (((0,), (0,)), ((), ())), preferred_element_type=jnp.float32).astype(jnp.bfloat16)
    weight_grad = lax.dot_general(features, value_grad, (((0,), (0,)), ((), ())), preferred_element_type=jnp.float32)
    return hidden, new_state, new_norm, weight_grad


def reference(stream_map, lengths, features, query_rows, key_rows, log_forget, in_gate, value_weight, state, norm_state, cotangent):
    slot_count = stream_map.shape[0]
    source_slot = jnp.zeros((slot_count,), jnp.int32).at[stream_map].set(jnp.arange(slot_count, dtype=jnp.int32))
    start_state = state[source_slot]
    start_norm = norm_state[source_slot]

    def one_stream(grad_sum, inputs):
        length, feats_now, query_now, key_now, forget_now, gate_now, state_now, norm_now, cot_now = inputs
        hidden_parts, state_parts, norm_parts, grad_parts = [], [], [], []
        for head_index in range(HEAD_COUNT):
            lower = head_index * DH
            result = head_pass(feats_now, value_weight[:, lower:lower + DH], query_now[:, lower:lower + DH],
                               key_now[:, lower:lower + DH], forget_now[:, head_index], gate_now[:, head_index],
                               length, state_now[head_index], norm_now[head_index], cot_now[:, lower:lower + DH])
            hidden_parts.append(result[0])
            state_parts.append(result[1])
            norm_parts.append(result[2])
            grad_parts.append(result[3])
        grad_sum = grad_sum + jnp.concatenate(grad_parts, axis=1)
        return grad_sum, (jnp.concatenate(hidden_parts, axis=1), jnp.stack(state_parts), jnp.stack(norm_parts))

    initial = jnp.zeros((DIN, HEAD_COUNT * DH), jnp.float32)
    grad_total, stacked = lax.scan(one_stream, initial, (lengths, features, query_rows, key_rows, log_forget, in_gate, start_state, start_norm, cotangent))
    return stacked[0], stacked[1], stacked[2], grad_total
```

```python
import jax
import jax.numpy as jnp
from jax import lax
from jax.sharding import PartitionSpec as P


def migrate(stream_map, state, norm_state):
    slot_count = lax.axis_size("dp")
    head_width = state.shape[-1]
    row_part = head_width // slot_count
    blocks = state[0, 0].astype(jnp.bfloat16).reshape(slot_count, row_part, head_width)
    spread = lax.all_to_all(blocks, "dp", split_axis=0, concat_axis=0, tiled=True)
    norms = lax.all_gather(norm_state[0, 0], "dp", axis=0, tiled=False)
    chosen = jnp.arange(slot_count, dtype=jnp.int32)[:, None] == stream_map[None, :]
    picked = jnp.einsum(
        "ps,src->prc",
        chosen.astype(jnp.bfloat16),
        spread,
        preferred_element_type=jnp.float32,
    ).astype(jnp.bfloat16)
    returned = lax.all_to_all(picked, "dp", split_axis=0, concat_axis=0, tiled=True)
    mine = lax.axis_index("dp") == stream_map
    start_norm = jnp.sum(jnp.where(mine[:, None], norms, 0.0), axis=0)
    return (returned.reshape(head_width, head_width), start_norm)


def window_terms(feature_all, value_weight, queries, key_vectors, forget_logs, gate_logs, length):
    window = queries.shape[0]
    head_width = queries.shape[1]
    values = jnp.dot(
        feature_all,
        lax.all_gather(value_weight, "dp", axis=0, tiled=True),
        preferred_element_type=jnp.float32,
    ).astype(jnp.bfloat16)
    position = jnp.arange(window, dtype=jnp.int32)
    live_mask = (position < length).astype(jnp.float32)
    weights_in = jnp.exp(gate_logs) * live_mask
    causal = position[:, None] >= position[None, :]
    decays = jnp.sum(jnp.where(causal, (forget_logs * live_mask)[None, :], 0.0), axis=1)
    gap_logs = jnp.where(causal, decays[:, None] - decays[None, :], -1e30)
    mixing = jnp.exp(gap_logs) * weights_in[None, :]
    scores = lax.dot_general(
        queries, key_vectors, (((1,), (1,)), ((), ())), preferred_element_type=jnp.float32
    ) * head_width ** (-0.5)
    combined = mixing * scores
    combined_low = combined.astype(jnp.bfloat16)
    local_numer = jnp.dot(combined_low, values, preferred_element_type=jnp.float32)
    local_inner = jnp.sum(combined, axis=1)
    return (values, live_mask, decays, weights_in, combined_low, local_numer, local_inner)


def on_device(
    stream_map,
    lengths,
    features,
    query_rows,
    key_rows,
    log_forget,
    in_gate,
    value_weight,
    state,
    norm_state,
    cotangent,
):
    feature_all = lax.all_gather(features, "mp", axis=2, tiled=True)[0]
    queries = query_rows[0]
    key_vectors = key_rows[0]
    head_width = queries.shape[1]
    window = queries.shape[0]
    start_state, start_norm = migrate(stream_map, state, norm_state)
    terms = window_terms(
        feature_all,
        value_weight,
        queries,
        key_vectors,
        log_forget[0, :, 0],
        in_gate[0, :, 0],
        lengths[0],
    )
    values, live_mask, decays, weights_in, combined_low, local_numer, local_inner = terms
    carried = jnp.exp(decays)
    query_wide = queries.astype(jnp.float32)
    from_state = jnp.dot(queries, start_state, preferred_element_type=jnp.float32)
    numer = carried[:, None] * from_state + local_numer
    inner_dot = (
        carried * jnp.sum(query_wide * start_norm[None, :], axis=1) + local_inner
    )
    denominator = jnp.maximum(jnp.abs(inner_dot), 1.0)
    hidden = (numer / denominator[:, None] * live_mask[:, None]).astype(jnp.bfloat16)
    final_decay = decays[window - 1]
    tail_weight = jnp.exp(final_decay - decays) * weights_in * head_width ** (-0.5)
    key_scaled = (key_vectors.astype(jnp.float32) * tail_weight[:, None]).astype(jnp.bfloat16)
    new_state = jnp.exp(final_decay) * start_state.astype(jnp.float32) + lax.dot_general(
        key_scaled, values, (((0,), (0,)), ((), ())), preferred_element_type=jnp.float32
    )
    new_norm = jnp.exp(final_decay) * start_norm + jnp.sum(
        tail_weight[:, None] * key_vectors.astype(jnp.float32), axis=0
    )
    scaled = (cotangent[0].astype(jnp.float32) * (live_mask / denominator)[:, None]).astype(
        jnp.bfloat16
    )
    value_grad = lax.dot_general(
        combined_low, scaled, (((0,), (0,)), ((), ())), preferred_element_type=jnp.float32
    ).astype(jnp.bfloat16)
    weight_grad = lax.psum_scatter(
        lax.dot_general(
            feature_all, value_grad, (((0,), (0,)), ((), ())), preferred_element_type=jnp.float32
        ),
        "dp",
        scatter_dimension=0,
        tiled=True,
    )
    return (hidden[None], new_state[None, None], new_norm[None, None], weight_grad)


def solution(mesh):
    return jax.shard_map(
        on_device,
        mesh=mesh,
        in_specs=(
            P(),
            P("dp"),
            P("dp", None, "mp"),
            P("dp", None, "mp"),
            P("dp", None, "mp"),
            P("dp", None, "mp"),
            P("dp", None, "mp"),
            P("dp", "mp"),
            P("dp", "mp", None, None),
            P("dp", "mp", None),
            P("dp", None, "mp"),
        ),
        out_specs=(
            P("dp", None, "mp"),
            P("dp", "mp", None, None),
            P("dp", "mp", None),
            P("dp", "mp"),
        ),
        check_vma=False,
    )
```

```python
import functools

import jax
import jax.numpy as jnp
from jax import lax
from jax.experimental import pallas as pl
from jax.experimental.pallas import tpu as pltpu
from jax.sharding import PartitionSpec as P


def migrate(stream_map, state, norm_state):
    slot_count = lax.axis_size("dp")
    head_width = state.shape[-1]
    row_part = head_width // slot_count
    blocks = state[0, 0].astype(jnp.bfloat16).reshape(slot_count, row_part, head_width)
    spread = lax.all_to_all(blocks, "dp", split_axis=0, concat_axis=0, tiled=True)
    norms = lax.all_gather(norm_state[0, 0], "dp", axis=0, tiled=False)
    chosen = jnp.arange(slot_count, dtype=jnp.int32)[:, None] == stream_map[None, :]
    picked = jnp.einsum(
        "ps,src->prc",
        chosen.astype(jnp.bfloat16),
        spread,
        preferred_element_type=jnp.float32,
    ).astype(jnp.bfloat16)
    returned = lax.all_to_all(picked, "dp", split_axis=0, concat_axis=0, tiled=True)
    mine = lax.axis_index("dp") == stream_map
    start_norm = jnp.sum(jnp.where(mine[:, None], norms, 0.0), axis=0)
    return (returned.reshape(head_width, head_width), start_norm)


def window_terms(feature_all, value_weight, queries, key_vectors, forget_logs, gate_logs, length):
    window = queries.shape[0]
    head_width = queries.shape[1]
    values = jnp.dot(
        feature_all,
        lax.all_gather(value_weight, "dp", axis=0, tiled=True),
        preferred_element_type=jnp.float32,
    ).astype(jnp.bfloat16)
    position = jnp.arange(window, dtype=jnp.int32)
    live_mask = (position < length).astype(jnp.float32)
    weights_in = jnp.exp(gate_logs) * live_mask
    causal = position[:, None] >= position[None, :]
    decays = jnp.sum(jnp.where(causal, (forget_logs * live_mask)[None, :], 0.0), axis=1)
    gap_logs = jnp.where(causal, decays[:, None] - decays[None, :], -1e30)
    mixing = jnp.exp(gap_logs) * weights_in[None, :]
    scores = lax.dot_general(
        queries, key_vectors, (((1,), (1,)), ((), ())), preferred_element_type=jnp.float32
    ) * head_width ** (-0.5)
    combined = mixing * scores
    combined_low = combined.astype(jnp.bfloat16)
    local_numer = jnp.dot(combined_low, values, preferred_element_type=jnp.float32)
    local_inner = jnp.sum(combined, axis=1)
    return (values, live_mask, decays, weights_in, combined_low, local_numer, local_inner)


def with_collectives(
    stream_map,
    lengths,
    features,
    query_rows,
    key_rows,
    log_forget,
    in_gate,
    value_weight,
    state,
    norm_state,
    cotangent,
):
    feature_all = lax.all_gather(features, "mp", axis=2, tiled=True)[0]
    queries = query_rows[0]
    key_vectors = key_rows[0]
    head_width = queries.shape[1]
    window = queries.shape[0]
    start_state, start_norm = migrate(stream_map, state, norm_state)
    terms = window_terms(
        feature_all,
        value_weight,
        queries,
        key_vectors,
        log_forget[0, :, 0],
        in_gate[0, :, 0],
        lengths[0],
    )
    values, live_mask, decays, weights_in, combined_low, local_numer, local_inner = terms
    carried = jnp.exp(decays)
    query_wide = queries.astype(jnp.float32)
    from_state = jnp.dot(queries, start_state, preferred_element_type=jnp.float32)
    numer = carried[:, None] * from_state + local_numer
    inner_dot = (
        carried * jnp.sum(query_wide * start_norm[None, :], axis=1) + local_inner
    )
    denominator = jnp.maximum(jnp.abs(inner_dot), 1.0)
    hidden = (numer / denominator[:, None] * live_mask[:, None]).astype(jnp.bfloat16)
    final_decay = decays[window - 1]
    tail_weight = jnp.exp(final_decay - decays) * weights_in * head_width ** (-0.5)
    key_scaled = (key_vectors.astype(jnp.float32) * tail_weight[:, None]).astype(jnp.bfloat16)
    new_state = jnp.exp(final_decay) * start_state.astype(jnp.float32) + lax.dot_general(
        key_scaled, values, (((0,), (0,)), ((), ())), preferred_element_type=jnp.float32
    )
    new_norm = jnp.exp(final_decay) * start_norm + jnp.sum(
        tail_weight[:, None] * key_vectors.astype(jnp.float32), axis=0
    )
    scaled = (cotangent[0].astype(jnp.float32) * (live_mask / denominator)[:, None]).astype(
        jnp.bfloat16
    )
    value_grad = lax.dot_general(
        combined_low, scaled, (((0,), (0,)), ((), ())), preferred_element_type=jnp.float32
    ).astype(jnp.bfloat16)
    weight_grad = lax.psum_scatter(
        lax.dot_general(
            feature_all, value_grad, (((0,), (0,)), ((), ())), preferred_element_type=jnp.float32
        ),
        "dp",
        scatter_dimension=0,
        tiled=True,
    )
    return (hidden[None], new_state[None, None], new_norm[None, None], weight_grad)


def remote(src, dst, send_sem, recv_sem, peer):
    return pltpu.make_async_remote_copy(
        src_ref=src,
        dst_ref=dst,
        send_sem=send_sem,
        recv_sem=recv_sem,
        device_id=peer,
        device_id_type=pl.DeviceIdType.MESH,
    )


def window_kernel(
    slots,
    heads,
    map_ref,
    length_ref,
    f_ref,
    q_ref,
    k_ref,
    forget_ref,
    gate_ref,
    w_ref,
    s_ref,
    n_ref,
    cot_ref,
    hidden_ref,
    state_ref,
    norm_ref,
    grad_ref,
    fbuf,
    wbuf,
    nbuf,
    sblk,
    s1,
    picked,
    s2,
    part,
    psend,
    yrecv,
    zsend,
    zrecv,
    f_sems,
    n_sems,
    s1_sems,
    s2_sems,
    wz_sems,
    wy_sems,
    y_sems,
    z_sems,
):
    lines = slots // 2
    me = lax.axis_index("dp")
    head = lax.axis_index("mp")
    z, y = me // 2, lax.rem(me, 2)
    other = 1 - y
    pair = {"dp": z * 2 + other}

    def ahead(k):
        return lax.rem(me + k, slots)

    def line_ahead(k):
        return lax.rem(z + k, lines)

    barrier = pltpu.get_barrier_semaphore()
    for k in range(1, slots):
        pl.semaphore_signal(
            barrier, inc=1, device_id={"dp": ahead(k)}, device_id_type=pl.DeviceIdType.MESH
        )
    for k in range(1, heads):
        pl.semaphore_signal(
            barrier,
            inc=1,
            device_id={"mp": lax.rem(head + k, heads)},
            device_id_type=pl.DeviceIdType.MESH,
        )
    pl.semaphore_wait(barrier, slots + heads - 2)

    norm_copies = [
        remote(n_ref, nbuf.at[me], n_sems.at[0, k], n_sems.at[1, k], {"dp": ahead(k)})
        for k in range(1, slots)
    ]
    feature_copies = [
        remote(
            f_ref,
            fbuf.at[head],
            f_sems.at[0, k],
            f_sems.at[1, k],
            {"mp": lax.rem(head + k, heads)},
        )
        for k in range(1, heads)
    ]
    for copy in norm_copies + feature_copies:
        copy.start()
    sblk[...] = s_ref[...].astype(jnp.bfloat16)
    spread_copies = [
        remote(
            sblk.at[ahead(k)], s1.at[me], s1_sems.at[0, k], s1_sems.at[1, k], {"dp": ahead(k)}
        )
        for k in range(1, slots)
    ]
    for copy in spread_copies:
        copy.start()
    line_copies = [
        remote(
            w_ref,
            wbuf.at[me],
            wz_sems.at[0, k],
            wz_sems.at[1, k],
            {"dp": line_ahead(k) * 2 + y},
        )
        for k in range(1, lines)
    ]
    pair_copies = [remote(w_ref, wbuf.at[me], wy_sems.at[0, 0], wy_sems.at[1, 0], pair)]
    pair_copies[0].start()
    for copy in line_copies:
        copy.start()

    nbuf[me] = n_ref[...]
    fbuf[head] = f_ref[...]
    wbuf[me] = w_ref[...]
    s1[me] = sblk[me]

    window, width = q_ref.shape
    length = length_ref[0]
    row = lax.broadcasted_iota(jnp.int32, (window, window), 0)
    column = lax.broadcasted_iota(jnp.int32, (window, window), 1)
    causal = row >= column
    diagonal = row == column
    live = (lax.broadcasted_iota(jnp.int32, (window, 1), 0) < length).astype(jnp.float32)

    def as_row(x):
        return jnp.sum(jnp.where(diagonal, x, 0.0), axis=0, keepdims=True)

    weights_in = jnp.exp(gate_ref[...]) * live
    decays = jnp.sum(
        jnp.where(causal, as_row(forget_ref[...] * live), 0.0), axis=1, keepdims=True
    )
    mixing = jnp.exp(jnp.where(causal, decays - as_row(decays), -1e30)) * as_row(weights_in)
    scale = width**-0.5
    scores = lax.dot_general(
        q_ref[...], k_ref[...], (((1,), (1,)), ((), ())), preferred_element_type=jnp.float32
    )
    combined = mixing * (scores * scale)
    combined_low = combined.astype(jnp.bfloat16)
    carried = jnp.exp(decays)
    final_decay = decays[window - 1 : window, :]
    kept = jnp.exp(final_decay)
    tail = jnp.exp(final_decay - decays) * weights_in * scale
    key_wide = k_ref[...].astype(jnp.float32) * tail
    key_scaled = key_wide.astype(jnp.bfloat16)

    def source_of(p):
        found = jnp.int32(0)
        for s in range(slots):
            found = jnp.where(map_ref[s] == p, jnp.int32(s), found)
        return found

    for copy in norm_copies:
        copy.wait()
    start_norm = nbuf[source_of(me)]
    norm_ref[...] = kept * start_norm + jnp.sum(key_wide, axis=0, keepdims=True)
    inner = carried * jnp.sum(
        q_ref[...].astype(jnp.float32) * start_norm, axis=1, keepdims=True
    ) + jnp.sum(combined, axis=1, keepdims=True)
    denominator = jnp.maximum(jnp.abs(inner), 1.0)
    scaled = (cot_ref[...].astype(jnp.float32) * (live / denominator)).astype(jnp.bfloat16)
    value_grad = lax.dot_general(
        combined_low, scaled, (((0,), (0,)), ((), ())), preferred_element_type=jnp.float32
    ).astype(jnp.bfloat16)

    for copy in spread_copies:
        copy.wait()
    for p in range(slots):
        picked[p] = s1[source_of(p)]
    return_copies = [
        remote(
            picked.at[ahead(k)], s2.at[me], s2_sems.at[0, k], s2_sems.at[1, k], {"dp": ahead(k)}
        )
        for k in range(1, slots)
    ]
    for copy in return_copies:
        copy.start()
    s2[me] = picked[me]

    for copy in feature_copies:
        copy.wait()
    rows = grad_ref.shape[0]
    per_head = f_ref.shape[1] // rows
    for r in range(slots):
        lower = (r % per_head) * rows
        block = lax.dot_general(
            fbuf[r // per_head, :, lower : lower + rows],
            value_grad,
            (((0,), (0,)), ((), ())),
            preferred_element_type=jnp.float32,
        )
        part[r] = block
        psend[r] = block.astype(jnp.bfloat16)
    order = list(range(1, lines)) + [0]
    y_copies = [
        remote(
            psend.at[line_ahead(k) * 2 + other],
            yrecv.at[line_ahead(k)],
            y_sems.at[0, k],
            y_sems.at[1, k],
            pair,
        )
        for k in order
    ]
    for copy in y_copies:
        copy.start()

    for k in range(1, lines):
        line_copies[k - 1].wait()
        slot = lax.rem(z + lines - k, lines) * 2 + y
        forward = remote(wbuf.at[slot], wbuf.at[slot], wy_sems.at[0, k], wy_sems.at[1, k], pair)
        forward.start()
        pair_copies.append(forward)

    z_copies = []
    for k, copy in zip(order, y_copies):
        copy.wait()
        if k == 0:
            continue
        to = line_ahead(k)
        zsend[to] = (part[to * 2 + y] + yrecv[to].astype(jnp.float32)).astype(jnp.bfloat16)
        out = remote(
            zsend.at[to], zrecv.at[z], z_sems.at[0, k], z_sems.at[1, k], {"dp": to * 2 + y}
        )
        out.start()
        z_copies.append(out)

    for copy in return_copies:
        copy.wait()
    start_state = s2[...].reshape(width, width)
    from_state = carried * jnp.dot(
        q_ref[...], start_state, preferred_element_type=jnp.float32
    )
    for copy in pair_copies:
        copy.wait()
    depth = f_ref.shape[1]
    per_depth = depth // rows
    total = jnp.zeros((window, width), jnp.float32)
    for m in range(heads):
        total = total + jnp.dot(
            fbuf[m],
            wbuf[m * per_depth : (m + 1) * per_depth].reshape(depth, width),
            preferred_element_type=jnp.float32,
        )
    values = total.astype(jnp.bfloat16)
    numer = from_state + jnp.dot(combined_low, values, preferred_element_type=jnp.float32)
    hidden_ref[...] = (numer / denominator * live).astype(jnp.bfloat16)
    state_ref[...] = kept * start_state.astype(jnp.float32) + lax.dot_general(
        key_scaled, values, (((0,), (0,)), ((), ())), preferred_element_type=jnp.float32
    )
    grad = part[me] + yrecv[z].astype(jnp.float32)
    for k, copy in enumerate(z_copies):
        copy.wait()
        grad = grad + zrecv[lax.rem(z + lines - k - 1, lines)].astype(jnp.float32)
    grad_ref[...] = grad


def in_one_kernel(
    stream_map,
    lengths,
    features,
    query_rows,
    key_rows,
    log_forget,
    in_gate,
    value_weight,
    state,
    norm_state,
    cotangent,
):
    slots, heads = lax.axis_size("dp"), lax.axis_size("mp")
    window, width = query_rows.shape[1:]
    depth = features.shape[2]
    rows = value_weight.shape[0]
    row_part = width // slots
    lines = slots // 2
    low = jnp.bfloat16
    sems = pltpu.SemaphoreType.DMA
    vmem = pl.BlockSpec(memory_space=pltpu.VMEM)
    smem = pl.BlockSpec(memory_space=pltpu.SMEM)
    hidden, new_state, new_norm, grad = pl.pallas_call(
        functools.partial(window_kernel, slots, heads),
        out_shape=(
            jax.ShapeDtypeStruct((window, width), low),
            jax.ShapeDtypeStruct((width, width), jnp.float32),
            jax.ShapeDtypeStruct((1, width), jnp.float32),
            jax.ShapeDtypeStruct((rows, width), jnp.float32),
        ),
        in_specs=[smem, smem] + [vmem] * 9,
        out_specs=(vmem, vmem, vmem, vmem),
        scratch_shapes=[
            pltpu.VMEM((heads, window, depth), low),
            pltpu.VMEM((slots, rows, width), low),
            pltpu.VMEM((slots, 1, width), jnp.float32),
            pltpu.VMEM((slots, row_part, width), low),
            pltpu.VMEM((slots, row_part, width), low),
            pltpu.VMEM((slots, row_part, width), low),
            pltpu.VMEM((slots, row_part, width), low),
            pltpu.VMEM((slots, rows, width), jnp.float32),
            pltpu.VMEM((slots, rows, width), low),
            pltpu.VMEM((lines, rows, width), low),
            pltpu.VMEM((lines, rows, width), low),
            pltpu.VMEM((lines, rows, width), low),
            sems((2, heads)),
            sems((2, slots)),
            sems((2, slots)),
            sems((2, slots)),
            sems((2, lines)),
            sems((2, lines)),
            sems((2, lines)),
            sems((2, lines)),
        ],
        compiler_params=pltpu.CompilerParams(
            collective_id=0, has_side_effects=True, vmem_limit_bytes=48 * 1024 * 1024
        ),
    )(
        stream_map,
        lengths,
        features[0],
        query_rows[0],
        key_rows[0],
        log_forget[0],
        in_gate[0],
        value_weight,
        state[0, 0].reshape(slots, row_part, width),
        norm_state[0],
        cotangent[0],
    )
    return (hidden[None], new_state[None, None], new_norm[None], grad)


def on_device(*args):
    slots, heads = lax.axis_size("dp"), lax.axis_size("mp")
    depth, rows, width = args[2].shape[2], args[7].shape[0], args[8].shape[-1]
    whole_tiles = slots % 2 == 0 and width % (16 * slots) == 0 and rows % 128 == 0
    if whole_tiles and depth % rows == 0 and depth * heads == rows * slots:
        return in_one_kernel(*args)
    return with_collectives(*args)


def solution(mesh):
    return jax.shard_map(
        on_device,
        mesh=mesh,
        in_specs=(
            P(),
            P("dp"),
            P("dp", None, "mp"),
            P("dp", None, "mp"),
            P("dp", None, "mp"),
            P("dp", None, "mp"),
            P("dp", None, "mp"),
            P("dp", "mp"),
            P("dp", "mp", None, None),
            P("dp", "mp", None),
            P("dp", None, "mp"),
        ),
        out_specs=(
            P("dp", None, "mp"),
            P("dp", "mp", None, None),
            P("dp", "mp", None),
            P("dp", "mp"),
        ),
        check_vma=False,
    )
```

```python
import functools

import jax
import jax.numpy as jnp
from jax import lax
from jax.experimental import pallas as pl
from jax.experimental.pallas import tpu as pltpu
from jax.sharding import PartitionSpec as P


def migrate(stream_map, state, norm_state):
    slot_count = lax.axis_size("dp")
    head_width = state.shape[-1]
    row_part = head_width // slot_count
    blocks = state[0, 0].astype(jnp.bfloat16).reshape(slot_count, row_part, head_width)
    spread = lax.all_to_all(blocks, "dp", split_axis=0, concat_axis=0, tiled=True)
    norms = lax.all_gather(norm_state[0, 0], "dp", axis=0, tiled=False)
    chosen = jnp.arange(slot_count, dtype=jnp.int32)[:, None] == stream_map[None, :]
    picked = jnp.einsum(
        "ps,src->prc",
        chosen.astype(jnp.bfloat16),
        spread,
        preferred_element_type=jnp.float32,
    ).astype(jnp.bfloat16)
    returned = lax.all_to_all(picked, "dp", split_axis=0, concat_axis=0, tiled=True)
    mine = lax.axis_index("dp") == stream_map
    start_norm = jnp.sum(jnp.where(mine[:, None], norms, 0.0), axis=0)
    return (returned.reshape(head_width, head_width), start_norm)


def window_terms(feature_all, value_weight, queries, key_vectors, forget_logs, gate_logs, length):
    window = queries.shape[0]
    head_width = queries.shape[1]
    values = jnp.dot(
        feature_all,
        lax.all_gather(value_weight, "dp", axis=0, tiled=True),
        preferred_element_type=jnp.float32,
    ).astype(jnp.bfloat16)
    position = jnp.arange(window, dtype=jnp.int32)
    live_mask = (position < length).astype(jnp.float32)
    weights_in = jnp.exp(gate_logs) * live_mask
    causal = position[:, None] >= position[None, :]
    decays = jnp.sum(jnp.where(causal, (forget_logs * live_mask)[None, :], 0.0), axis=1)
    gap_logs = jnp.where(causal, decays[:, None] - decays[None, :], -1e30)
    mixing = jnp.exp(gap_logs) * weights_in[None, :]
    scores = lax.dot_general(
        queries, key_vectors, (((1,), (1,)), ((), ())), preferred_element_type=jnp.float32
    ) * head_width ** (-0.5)
    combined = mixing * scores
    combined_low = combined.astype(jnp.bfloat16)
    local_numer = jnp.dot(combined_low, values, preferred_element_type=jnp.float32)
    local_inner = jnp.sum(combined, axis=1)
    return (values, live_mask, decays, weights_in, combined_low, local_numer, local_inner)


def with_collectives(
    stream_map,
    lengths,
    features,
    query_rows,
    key_rows,
    log_forget,
    in_gate,
    value_weight,
    state,
    norm_state,
    cotangent,
):
    feature_all = lax.all_gather(features, "mp", axis=2, tiled=True)[0]
    queries = query_rows[0]
    key_vectors = key_rows[0]
    head_width = queries.shape[1]
    window = queries.shape[0]
    start_state, start_norm = migrate(stream_map, state, norm_state)
    terms = window_terms(
        feature_all,
        value_weight,
        queries,
        key_vectors,
        log_forget[0, :, 0],
        in_gate[0, :, 0],
        lengths[0],
    )
    values, live_mask, decays, weights_in, combined_low, local_numer, local_inner = terms
    carried = jnp.exp(decays)
    query_wide = queries.astype(jnp.float32)
    from_state = jnp.dot(queries, start_state, preferred_element_type=jnp.float32)
    numer = carried[:, None] * from_state + local_numer
    inner_dot = (
        carried * jnp.sum(query_wide * start_norm[None, :], axis=1) + local_inner
    )
    denominator = jnp.maximum(jnp.abs(inner_dot), 1.0)
    hidden = (numer / denominator[:, None] * live_mask[:, None]).astype(jnp.bfloat16)
    final_decay = decays[window - 1]
    tail_weight = jnp.exp(final_decay - decays) * weights_in * head_width ** (-0.5)
    key_scaled = (key_vectors.astype(jnp.float32) * tail_weight[:, None]).astype(jnp.bfloat16)
    new_state = jnp.exp(final_decay) * start_state.astype(jnp.float32) + lax.dot_general(
        key_scaled, values, (((0,), (0,)), ((), ())), preferred_element_type=jnp.float32
    )
    new_norm = jnp.exp(final_decay) * start_norm + jnp.sum(
        tail_weight[:, None] * key_vectors.astype(jnp.float32), axis=0
    )
    scaled = (cotangent[0].astype(jnp.float32) * (live_mask / denominator)[:, None]).astype(
        jnp.bfloat16
    )
    value_grad = lax.dot_general(
        combined_low, scaled, (((0,), (0,)), ((), ())), preferred_element_type=jnp.float32
    ).astype(jnp.bfloat16)
    weight_grad = lax.psum_scatter(
        lax.dot_general(
            feature_all, value_grad, (((0,), (0,)), ((), ())), preferred_element_type=jnp.float32
        ),
        "dp",
        scatter_dimension=0,
        tiled=True,
    )
    return (hidden[None], new_state[None, None], new_norm[None, None], weight_grad)


def remote(src, dst, send_sem, recv_sem, peer):
    return pltpu.make_async_remote_copy(
        src_ref=src,
        dst_ref=dst,
        send_sem=send_sem,
        recv_sem=recv_sem,
        device_id=peer,
        device_id_type=pl.DeviceIdType.MESH,
    )


def window_kernel(
    slots,
    heads,
    map_ref,
    length_ref,
    f_ref,
    q_hbm,
    k_hbm,
    forget_hbm,
    gate_hbm,
    w_ref,
    s_hbm,
    n_ref,
    cot_hbm,
    hidden_ref,
    state_ref,
    norm_ref,
    grad_ref,
    q_ref,
    k_ref,
    forget_ref,
    gate_ref,
    s_ref,
    cot_ref,
    fbuf,
    wbuf,
    nbuf,
    sblk,
    s1,
    picked,
    s2,
    part,
    psend,
    yrecv,
    zsend,
    zrecv,
    f_sems,
    n_sems,
    s1_sems,
    s2_sems,
    up_sems,
    down_sems,
    wy_sems,
    local_sems,
    y_sems,
    z_sems,
):
    lines = slots // 2
    me = lax.axis_index("dp")
    head = lax.axis_index("mp")
    z, y = me // 2, lax.rem(me, 2)
    other = 1 - y
    pair = {"dp": z * 2 + other}

    def ahead(k):
        return lax.rem(me + k, slots)

    def line_ahead(k):
        return lax.rem(z + k, lines)

    moves = (
        (s_hbm, s_ref),
        (q_hbm, q_ref),
        (k_hbm, k_ref),
        (forget_hbm, forget_ref),
        (gate_hbm, gate_ref),
        (cot_hbm, cot_ref),
        (f_ref, fbuf.at[head]),
        (w_ref, wbuf.at[me]),
        (n_ref, nbuf.at[me]),
    )
    fetches = [
        pltpu.make_async_copy(src, dst, local_sems.at[i]) for i, (src, dst) in enumerate(moves)
    ]
    for fetch in fetches:
        fetch.start()

    barrier = pltpu.get_barrier_semaphore()
    for k in range(1, slots):
        pl.semaphore_signal(
            barrier, inc=1, device_id={"dp": ahead(k)}, device_id_type=pl.DeviceIdType.MESH
        )
    for k in range(1, heads):
        pl.semaphore_signal(
            barrier,
            inc=1,
            device_id={"mp": lax.rem(head + k, heads)},
            device_id_type=pl.DeviceIdType.MESH,
        )
    pl.semaphore_wait(barrier, slots + heads - 2)

    norm_copies = [
        remote(n_ref, nbuf.at[me], n_sems.at[0, k], n_sems.at[1, k], {"dp": ahead(k)})
        for k in range(1, slots)
    ]
    feature_copies = [
        remote(
            f_ref,
            fbuf.at[head],
            f_sems.at[0, k],
            f_sems.at[1, k],
            {"mp": lax.rem(head + k, heads)},
        )
        for k in range(1, heads)
    ]
    for copy in norm_copies + feature_copies:
        copy.start()
    fetches[0].wait()
    sblk[...] = s_ref[...].astype(jnp.bfloat16)
    spread_copies = [
        remote(
            sblk.at[ahead(k)], s1.at[me], s1_sems.at[0, k], s1_sems.at[1, k], {"dp": ahead(k)}
        )
        for k in range(1, slots)
    ]
    for copy in spread_copies:
        copy.start()
    def on_line(i):
        return jnp.logical_and(i >= 0, i < lines)

    def hop(step, sems, j):
        slot = (z - step * j) * 2 + y
        to = {"dp": (z + step) * 2 + y}
        source = w_ref if j == 0 else wbuf.at[slot]
        return remote(source, wbuf.at[slot], sems.at[0, j], sems.at[1, j], to)

    def arrival(step, sems, j):
        slot = (z - step * (j + 1)) * 2 + y
        to = {"dp": (z - step) * 2 + y}
        return remote(wbuf.at[slot], wbuf.at[slot], sems.at[0, j], sems.at[1, j], to)

    def hand_over(line, own=False):
        slot = line * 2 + y
        source = w_ref if own else wbuf.at[slot]
        return remote(source, wbuf.at[slot], wy_sems.at[0, line], wy_sems.at[1, line], pair)

    directions = ((1, up_sems), (-1, down_sems))

    def pass_on(j):
        for step, sems in directions:

            @pl.when(on_line(z - step * (j + 1)))
            def _():
                arrival(step, sems, j).wait_recv()
                if j + 2 < lines:

                    @pl.when(on_line(z + step))
                    def _():
                        hop(step, sems, j + 1).start()

                hand_over(z - step * (j + 1)).start()

    for step, sems in directions:

        @pl.when(on_line(z + step))
        def _():
            hop(step, sems, 0).start()

    hand_over(z, True).start()

    s1[me] = sblk[me]
    for fetch in fetches[1:6]:
        fetch.wait()

    window, width = q_ref.shape
    length = length_ref[0]
    row = lax.broadcasted_iota(jnp.int32, (window, window), 0)
    column = lax.broadcasted_iota(jnp.int32, (window, window), 1)
    causal = row >= column
    diagonal = row == column
    live = (lax.broadcasted_iota(jnp.int32, (window, 1), 0) < length).astype(jnp.float32)
    live_row = (lax.broadcasted_iota(jnp.int32, (1, window), 1) < length).astype(jnp.float32)

    weights_row = jnp.exp(gate_ref[...]) * live_row
    weights_in = jnp.sum(jnp.where(diagonal, weights_row, 0.0), axis=1, keepdims=True)
    decays = jnp.sum(
        jnp.where(causal, forget_ref[...] * live_row, 0.0), axis=1, keepdims=True
    )
    decays_row = jnp.sum(jnp.where(diagonal, decays, 0.0), axis=0, keepdims=True)
    mixing = jnp.exp(jnp.where(causal, decays - decays_row, -1e30)) * weights_row
    scale = width**-0.5
    scores = lax.dot_general(
        q_ref[...], k_ref[...], (((1,), (1,)), ((), ())), preferred_element_type=jnp.float32
    )
    combined = mixing * (scores * scale)
    combined_low = combined.astype(jnp.bfloat16)
    carried = jnp.exp(decays)
    final_decay = decays[window - 1 : window, :]
    kept = jnp.exp(final_decay)
    tail = jnp.exp(final_decay - decays) * weights_in * scale
    key_wide = k_ref[...].astype(jnp.float32) * tail
    key_scaled = key_wide.astype(jnp.bfloat16)

    def source_of(p):
        found = jnp.int32(0)
        for s in range(slots):
            found = jnp.where(map_ref[s] == p, jnp.int32(s), found)
        return found

    fetches[8].wait()
    for copy in norm_copies:
        copy.wait()
    start_norm = nbuf[source_of(me)]
    norm_ref[...] = kept * start_norm + jnp.sum(key_wide, axis=0, keepdims=True)
    inner = carried * jnp.sum(
        q_ref[...].astype(jnp.float32) * start_norm, axis=1, keepdims=True
    ) + jnp.sum(combined, axis=1, keepdims=True)
    denominator = jnp.maximum(jnp.abs(inner), 1.0)
    scaled = (cot_ref[...].astype(jnp.float32) * (live / denominator)).astype(jnp.bfloat16)
    value_grad = lax.dot_general(
        combined_low, scaled, (((0,), (0,)), ((), ())), preferred_element_type=jnp.float32
    ).astype(jnp.bfloat16)

    pass_on(0)
    for copy in spread_copies:
        copy.wait()
    for p in range(slots):
        picked[p] = s1[source_of(p)]
    return_copies = [
        remote(
            picked.at[ahead(k)], s2.at[me], s2_sems.at[0, k], s2_sems.at[1, k], {"dp": ahead(k)}
        )
        for k in range(1, slots)
    ]
    for copy in return_copies:
        copy.start()
    s2[me] = picked[me]

    fetches[6].wait()
    for copy in feature_copies:
        copy.wait()
    rows = grad_ref.shape[0]
    per_head = f_ref.shape[1] // rows
    for r in range(slots):
        lower = (r % per_head) * rows
        block = lax.dot_general(
            fbuf[r // per_head, :, lower : lower + rows],
            value_grad,
            (((0,), (0,)), ((), ())),
            preferred_element_type=jnp.float32,
        )
        part[r] = block
        psend[r] = block.astype(jnp.bfloat16)
    order = list(range(1, lines)) + [0]
    y_copies = [
        remote(
            psend.at[line_ahead(k) * 2 + other],
            yrecv.at[line_ahead(k)],
            y_sems.at[0, k],
            y_sems.at[1, k],
            pair,
        )
        for k in order
    ]
    for copy in y_copies:
        copy.start()

    for j in range(1, lines - 1):
        pass_on(j)

    z_copies = []
    for k, copy in zip(order, y_copies):
        copy.wait()
        if k == 0:
            continue
        to = line_ahead(k)
        zsend[to] = (part[to * 2 + y] + yrecv[to].astype(jnp.float32)).astype(jnp.bfloat16)
        out = remote(
            zsend.at[to], zrecv.at[z], z_sems.at[0, k], z_sems.at[1, k], {"dp": to * 2 + y}
        )
        out.start()
        z_copies.append(out)

    for copy in return_copies:
        copy.wait()
    start_state = s2[...].reshape(width, width)
    from_state = carried * jnp.dot(
        q_ref[...], start_state, preferred_element_type=jnp.float32
    )
    fetches[7].wait()
    for line in range(lines):
        handed = remote(
            w_ref,
            wbuf.at[line * 2 + other],
            wy_sems.at[0, line],
            wy_sems.at[1, line],
            pair,
        )
        handed.wait()
    for j in range(lines - 1):
        for step, sems in directions:

            @pl.when(jnp.logical_and(on_line(z + step), on_line(z - step * j)))
            def _():
                hop(step, sems, j).wait_send()

    depth = f_ref.shape[1]
    per_depth = depth // rows
    total = jnp.zeros((window, width), jnp.float32)
    for m in range(heads):
        total = total + jnp.dot(
            fbuf[m],
            wbuf[m * per_depth : (m + 1) * per_depth].reshape(depth, width),
            preferred_element_type=jnp.float32,
        )
    values = total.astype(jnp.bfloat16)
    numer = from_state + jnp.dot(combined_low, values, preferred_element_type=jnp.float32)
    hidden_ref[...] = (numer / denominator * live).astype(jnp.bfloat16)
    state_ref[...] = kept * start_state.astype(jnp.float32) + lax.dot_general(
        key_scaled, values, (((0,), (0,)), ((), ())), preferred_element_type=jnp.float32
    )
    grad = part[me] + yrecv[z].astype(jnp.float32)
    for k, copy in enumerate(z_copies):
        copy.wait()
        grad = grad + zrecv[lax.rem(z + lines - k - 1, lines)].astype(jnp.float32)
    grad_ref[...] = grad


def in_one_kernel(
    stream_map,
    lengths,
    features,
    query_rows,
    key_rows,
    log_forget,
    in_gate,
    value_weight,
    state,
    norm_state,
    cotangent,
):
    slots, heads = lax.axis_size("dp"), lax.axis_size("mp")
    window, width = query_rows.shape[1:]
    depth = features.shape[2]
    rows = value_weight.shape[0]
    row_part = width // slots
    lines = slots // 2
    low = jnp.bfloat16
    sems = pltpu.SemaphoreType.DMA
    vmem = pl.BlockSpec(memory_space=pltpu.VMEM)
    smem = pl.BlockSpec(memory_space=pltpu.SMEM)
    hidden, new_state, new_norm, grad = pl.pallas_call(
        functools.partial(window_kernel, slots, heads),
        out_shape=(
            jax.ShapeDtypeStruct((window, width), low),
            jax.ShapeDtypeStruct((width, width), jnp.float32),
            jax.ShapeDtypeStruct((1, width), jnp.float32),
            jax.ShapeDtypeStruct((rows, width), jnp.float32),
        ),
        in_specs=[smem, smem] + [pl.BlockSpec(memory_space=pltpu.HBM)] * 9,
        out_specs=(vmem, vmem, vmem, vmem),
        scratch_shapes=[
            pltpu.VMEM((window, width), low),
            pltpu.VMEM((window, width), low),
            pltpu.VMEM((1, window), jnp.float32),
            pltpu.VMEM((1, window), jnp.float32),
            pltpu.VMEM((slots, row_part, width), jnp.float32),
            pltpu.VMEM((window, width), low),
            pltpu.VMEM((heads, window, depth), low),
            pltpu.VMEM((slots, rows, width), low),
            pltpu.VMEM((slots, 1, width), jnp.float32),
            pltpu.VMEM((slots, row_part, width), low),
            pltpu.VMEM((slots, row_part, width), low),
            pltpu.VMEM((slots, row_part, width), low),
            pltpu.VMEM((slots, row_part, width), low),
            pltpu.VMEM((slots, rows, width), jnp.float32),
            pltpu.VMEM((slots, rows, width), low),
            pltpu.VMEM((lines, rows, width), low),
            pltpu.VMEM((lines, rows, width), low),
            pltpu.VMEM((lines, rows, width), low),
            sems((2, heads)),
            sems((2, slots)),
            sems((2, slots)),
            sems((2, slots)),
            sems((2, lines)),
            sems((2, lines)),
            sems((2, lines)),
            sems((9,)),
            sems((2, lines)),
            sems((2, lines)),
        ],
        compiler_params=pltpu.CompilerParams(
            collective_id=0, has_side_effects=True, vmem_limit_bytes=60 * 1024 * 1024
        ),
    )(
        stream_map,
        lengths,
        features[0],
        query_rows[0],
        key_rows[0],
        log_forget.reshape(1, window),
        in_gate.reshape(1, window),
        value_weight,
        state[0, 0].reshape(slots, row_part, width),
        norm_state[0],
        cotangent[0],
    )
    return (hidden[None], new_state[None, None], new_norm[None], grad)


def on_device(*args):
    slots, heads = lax.axis_size("dp"), lax.axis_size("mp")
    depth, rows, width = args[2].shape[2], args[7].shape[0], args[8].shape[-1]
    whole_tiles = slots % 2 == 0 and width % (16 * slots) == 0 and rows % 128 == 0
    if whole_tiles and depth % rows == 0 and depth * heads == rows * slots:
        return in_one_kernel(*args)
    return with_collectives(*args)


def solution(mesh):
    return jax.shard_map(
        on_device,
        mesh=mesh,
        in_specs=(
            P(),
            P("dp"),
            P("dp", None, "mp"),
            P("dp", None, "mp"),
            P("dp", None, "mp"),
            P("dp", None, "mp"),
            P("dp", None, "mp"),
            P("dp", "mp"),
            P("dp", "mp", None, None),
            P("dp", "mp", None),
            P("dp", None, "mp"),
        ),
        out_specs=(
            P("dp", None, "mp"),
            P("dp", "mp", None, None),
            P("dp", "mp", None),
            P("dp", "mp"),
        ),
        check_vma=False,
    )
```

```python
import functools

import jax
import jax.numpy as jnp
from jax import lax
from jax.experimental import pallas as pl
from jax.experimental.pallas import tpu as pltpu
from jax.sharding import PartitionSpec as P


def migrate(stream_map, state, norm_state):
    slot_count = lax.axis_size("dp")
    head_width = state.shape[-1]
    row_part = head_width // slot_count
    blocks = state[0, 0].astype(jnp.bfloat16).reshape(slot_count, row_part, head_width)
    spread = lax.all_to_all(blocks, "dp", split_axis=0, concat_axis=0, tiled=True)
    norms = lax.all_gather(norm_state[0, 0], "dp", axis=0, tiled=False)
    chosen = jnp.arange(slot_count, dtype=jnp.int32)[:, None] == stream_map[None, :]
    picked = jnp.einsum(
        "ps,src->prc",
        chosen.astype(jnp.bfloat16),
        spread,
        preferred_element_type=jnp.float32,
    ).astype(jnp.bfloat16)
    returned = lax.all_to_all(picked, "dp", split_axis=0, concat_axis=0, tiled=True)
    mine = lax.axis_index("dp") == stream_map
    start_norm = jnp.sum(jnp.where(mine[:, None], norms, 0.0), axis=0)
    return (returned.reshape(head_width, head_width), start_norm)


def window_terms(feature_all, value_weight, queries, key_vectors, forget_logs, gate_logs, length):
    window = queries.shape[0]
    head_width = queries.shape[1]
    values = jnp.dot(
        feature_all,
        lax.all_gather(value_weight, "dp", axis=0, tiled=True),
        preferred_element_type=jnp.float32,
    ).astype(jnp.bfloat16)
    position = jnp.arange(window, dtype=jnp.int32)
    live_mask = (position < length).astype(jnp.float32)
    weights_in = jnp.exp(gate_logs) * live_mask
    causal = position[:, None] >= position[None, :]
    decays = jnp.sum(jnp.where(causal, (forget_logs * live_mask)[None, :], 0.0), axis=1)
    gap_logs = jnp.where(causal, decays[:, None] - decays[None, :], -1e30)
    mixing = jnp.exp(gap_logs) * weights_in[None, :]
    scores = lax.dot_general(
        queries, key_vectors, (((1,), (1,)), ((), ())), preferred_element_type=jnp.float32
    ) * head_width ** (-0.5)
    combined = mixing * scores
    combined_low = combined.astype(jnp.bfloat16)
    local_numer = jnp.dot(combined_low, values, preferred_element_type=jnp.float32)
    local_inner = jnp.sum(combined, axis=1)
    return (values, live_mask, decays, weights_in, combined_low, local_numer, local_inner)


def with_collectives(
    stream_map,
    lengths,
    features,
    query_rows,
    key_rows,
    log_forget,
    in_gate,
    value_weight,
    state,
    norm_state,
    cotangent,
):
    feature_all = lax.all_gather(features, "mp", axis=2, tiled=True)[0]
    queries = query_rows[0]
    key_vectors = key_rows[0]
    head_width = queries.shape[1]
    window = queries.shape[0]
    start_state, start_norm = migrate(stream_map, state, norm_state)
    terms = window_terms(
        feature_all,
        value_weight,
        queries,
        key_vectors,
        log_forget[0, :, 0],
        in_gate[0, :, 0],
        lengths[0],
    )
    values, live_mask, decays, weights_in, combined_low, local_numer, local_inner = terms
    carried = jnp.exp(decays)
    query_wide = queries.astype(jnp.float32)
    from_state = jnp.dot(queries, start_state, preferred_element_type=jnp.float32)
    numer = carried[:, None] * from_state + local_numer
    inner_dot = (
        carried * jnp.sum(query_wide * start_norm[None, :], axis=1) + local_inner
    )
    denominator = jnp.maximum(jnp.abs(inner_dot), 1.0)
    hidden = (numer / denominator[:, None] * live_mask[:, None]).astype(jnp.bfloat16)
    final_decay = decays[window - 1]
    tail_weight = jnp.exp(final_decay - decays) * weights_in * head_width ** (-0.5)
    key_scaled = (key_vectors.astype(jnp.float32) * tail_weight[:, None]).astype(jnp.bfloat16)
    new_state = jnp.exp(final_decay) * start_state.astype(jnp.float32) + lax.dot_general(
        key_scaled, values, (((0,), (0,)), ((), ())), preferred_element_type=jnp.float32
    )
    new_norm = jnp.exp(final_decay) * start_norm + jnp.sum(
        tail_weight[:, None] * key_vectors.astype(jnp.float32), axis=0
    )
    scaled = (cotangent[0].astype(jnp.float32) * (live_mask / denominator)[:, None]).astype(
        jnp.bfloat16
    )
    value_grad = lax.dot_general(
        combined_low, scaled, (((0,), (0,)), ((), ())), preferred_element_type=jnp.float32
    ).astype(jnp.bfloat16)
    weight_grad = lax.psum_scatter(
        lax.dot_general(
            feature_all, value_grad, (((0,), (0,)), ((), ())), preferred_element_type=jnp.float32
        ),
        "dp",
        scatter_dimension=0,
        tiled=True,
    )
    return (hidden[None], new_state[None, None], new_norm[None, None], weight_grad)


def remote(src, dst, send_sem, recv_sem, peer):
    return pltpu.make_async_remote_copy(
        src_ref=src,
        dst_ref=dst,
        send_sem=send_sem,
        recv_sem=recv_sem,
        device_id=peer,
        device_id_type=pl.DeviceIdType.MESH,
    )


def window_kernel(
    slots,
    heads,
    map_ref,
    length_ref,
    f_ref,
    q_hbm,
    k_hbm,
    forget_hbm,
    gate_hbm,
    w_ref,
    s_hbm,
    n_ref,
    cot_hbm,
    hidden_ref,
    state_ref,
    norm_ref,
    grad_ref,
    q_ref,
    k_ref,
    forget_ref,
    gate_ref,
    s_ref,
    cot_ref,
    fbuf,
    wbuf,
    nbuf,
    sblk,
    s1,
    picked,
    s2,
    part,
    psend,
    yrecv,
    zsend,
    zrecv,
    f_sems,
    n_sems,
    s1_sems,
    s2_sems,
    up_sems,
    down_sems,
    wy_sems,
    local_sems,
    y_sems,
    z_sems,
):
    lines = slots // 2
    me = lax.axis_index("dp")
    head = lax.axis_index("mp")
    z, y = me // 2, lax.rem(me, 2)
    other = 1 - y
    pair = {"dp": z * 2 + other}

    def ahead(k):
        return lax.rem(me + k, slots)

    def line_ahead(k):
        return lax.rem(z + k, lines)

    moves = (
        (s_hbm, s_ref),
        (q_hbm, q_ref),
        (k_hbm, k_ref),
        (forget_hbm, forget_ref),
        (gate_hbm, gate_ref),
        (cot_hbm, cot_ref),
        (f_ref, fbuf.at[head]),
        (w_ref, wbuf.at[me]),
        (n_ref, nbuf.at[me]),
    )
    fetches = [
        pltpu.make_async_copy(src, dst, local_sems.at[i]) for i, (src, dst) in enumerate(moves)
    ]
    for fetch in fetches:
        fetch.start()

    barrier = pltpu.get_barrier_semaphore()
    for k in range(1, slots):
        pl.semaphore_signal(
            barrier, inc=1, device_id={"dp": ahead(k)}, device_id_type=pl.DeviceIdType.MESH
        )
    for k in range(1, heads):
        pl.semaphore_signal(
            barrier,
            inc=1,
            device_id={"mp": lax.rem(head + k, heads)},
            device_id_type=pl.DeviceIdType.MESH,
        )
    pl.semaphore_wait(barrier, slots + heads - 2)

    norm_copies = [
        remote(n_ref, nbuf.at[me], n_sems.at[0, k], n_sems.at[1, k], {"dp": ahead(k)})
        for k in range(1, slots)
    ]
    feature_copies = [
        remote(
            f_ref,
            fbuf.at[head],
            f_sems.at[0, k],
            f_sems.at[1, k],
            {"mp": lax.rem(head + k, heads)},
        )
        for k in range(1, heads)
    ]
    for copy in norm_copies + feature_copies:
        copy.start()
    fetches[0].wait()
    sblk[...] = s_ref[...].astype(jnp.bfloat16)
    spread_copies = [
        remote(
            sblk.at[ahead(k)], s1.at[me], s1_sems.at[0, k], s1_sems.at[1, k], {"dp": ahead(k)}
        )
        for k in range(1, slots)
    ]
    for copy in spread_copies:
        copy.start()
    def on_line(i):
        return jnp.logical_and(i >= 0, i < lines)

    def hop(step, sems, j):
        slot = (z - step * j) * 2 + y
        to = {"dp": (z + step) * 2 + y}
        source = w_ref if j == 0 else wbuf.at[slot]
        return remote(source, wbuf.at[slot], sems.at[0, j], sems.at[1, j], to)

    def arrival(step, sems, j):
        slot = (z - step * (j + 1)) * 2 + y
        to = {"dp": (z - step) * 2 + y}
        return remote(wbuf.at[slot], wbuf.at[slot], sems.at[0, j], sems.at[1, j], to)

    def hand_over(line, own=False):
        slot = line * 2 + y
        source = w_ref if own else wbuf.at[slot]
        return remote(source, wbuf.at[slot], wy_sems.at[0, line], wy_sems.at[1, line], pair)

    directions = ((1, up_sems), (-1, down_sems))

    def pass_on(j):
        for step, sems in directions:

            @pl.when(on_line(z - step * (j + 1)))
            def _():
                arrival(step, sems, j).wait_recv()
                if j + 2 < lines:

                    @pl.when(on_line(z + step))
                    def _():
                        hop(step, sems, j + 1).start()

    def hand_on(j):
        for step, _ in directions:

            @pl.when(on_line(z - step * (j + 1)))
            def _():
                hand_over(z - step * (j + 1)).start()

    for step, sems in directions:

        @pl.when(on_line(z + step))
        def _():
            hop(step, sems, 0).start()

    hand_over(z, True).start()

    s1[me] = sblk[me]
    for fetch in fetches[1:6]:
        fetch.wait()

    window, width = q_ref.shape
    length = length_ref[0]
    row = lax.broadcasted_iota(jnp.int32, (window, window), 0)
    column = lax.broadcasted_iota(jnp.int32, (window, window), 1)
    causal = row >= column
    diagonal = row == column
    live = (lax.broadcasted_iota(jnp.int32, (window, 1), 0) < length).astype(jnp.float32)
    live_row = (lax.broadcasted_iota(jnp.int32, (1, window), 1) < length).astype(jnp.float32)

    weights_row = jnp.exp(gate_ref[...]) * live_row
    weights_in = jnp.sum(jnp.where(diagonal, weights_row, 0.0), axis=1, keepdims=True)
    decays = jnp.sum(
        jnp.where(causal, forget_ref[...] * live_row, 0.0), axis=1, keepdims=True
    )
    decays_row = jnp.sum(jnp.where(diagonal, decays, 0.0), axis=0, keepdims=True)
    mixing = jnp.exp(jnp.where(causal, decays - decays_row, -1e30)) * weights_row
    scale = width**-0.5
    scores = lax.dot_general(
        q_ref[...], k_ref[...], (((1,), (1,)), ((), ())), preferred_element_type=jnp.float32
    )
    combined = mixing * (scores * scale)
    combined_low = combined.astype(jnp.bfloat16)
    carried = jnp.exp(decays)
    final_decay = decays[window - 1 : window, :]
    kept = jnp.exp(final_decay)
    tail = jnp.exp(final_decay - decays) * weights_in * scale
    key_wide = k_ref[...].astype(jnp.float32) * tail
    key_scaled = key_wide.astype(jnp.bfloat16)

    def source_of(p):
        found = jnp.int32(0)
        for s in range(slots):
            found = jnp.where(map_ref[s] == p, jnp.int32(s), found)
        return found

    fetches[8].wait()
    for copy in norm_copies:
        copy.wait()
    start_norm = nbuf[source_of(me)]
    norm_ref[...] = kept * start_norm + jnp.sum(key_wide, axis=0, keepdims=True)
    inner = carried * jnp.sum(
        q_ref[...].astype(jnp.float32) * start_norm, axis=1, keepdims=True
    ) + jnp.sum(combined, axis=1, keepdims=True)
    denominator = jnp.maximum(jnp.abs(inner), 1.0)
    scaled = (cot_ref[...].astype(jnp.float32) * (live / denominator)).astype(jnp.bfloat16)
    value_grad = lax.dot_general(
        combined_low, scaled, (((0,), (0,)), ((), ())), preferred_element_type=jnp.float32
    ).astype(jnp.bfloat16)

    pass_on(0)
    hand_on(0)
    for copy in spread_copies:
        copy.wait()
    for p in range(slots):
        picked[p] = s1[source_of(p)]
    return_copies = [
        remote(
            picked.at[ahead(k)], s2.at[me], s2_sems.at[0, k], s2_sems.at[1, k], {"dp": ahead(k)}
        )
        for k in range(1, slots)
    ]
    for copy in return_copies:
        copy.start()
    s2[me] = picked[me]

    fetches[6].wait()
    for copy in feature_copies:
        copy.wait()
    rows = grad_ref.shape[0]
    per_head = f_ref.shape[1] // rows
    for r in range(slots):
        lower = (r % per_head) * rows
        block = lax.dot_general(
            fbuf[r // per_head, :, lower : lower + rows],
            value_grad,
            (((0,), (0,)), ((), ())),
            preferred_element_type=jnp.float32,
        )
        part[r] = block
        psend[r] = block.astype(jnp.bfloat16)
    order = list(range(1, lines)) + [0]
    y_copies = [
        remote(
            psend.at[line_ahead(k) * 2 + other],
            yrecv.at[line_ahead(k)],
            y_sems.at[0, k],
            y_sems.at[1, k],
            pair,
        )
        for k in order
    ]
    for copy in y_copies:
        copy.start()

    for j in range(1, lines - 1):
        pass_on(j)

    z_copies = []
    for k, copy in zip(order, y_copies):
        copy.wait()
        if k == 0:
            continue
        to = line_ahead(k)
        zsend[to] = (part[to * 2 + y] + yrecv[to].astype(jnp.float32)).astype(jnp.bfloat16)
        out = remote(
            zsend.at[to], zrecv.at[z], z_sems.at[0, k], z_sems.at[1, k], {"dp": to * 2 + y}
        )
        out.start()
        z_copies.append(out)
    for j in range(1, lines - 1):
        hand_on(j)

    for copy in return_copies:
        copy.wait()
    start_state = s2[...].reshape(width, width)
    from_state = carried * jnp.dot(
        q_ref[...], start_state, preferred_element_type=jnp.float32
    )
    fetches[7].wait()
    for line in range(lines):
        handed = remote(
            w_ref,
            wbuf.at[line * 2 + other],
            wy_sems.at[0, line],
            wy_sems.at[1, line],
            pair,
        )
        handed.wait()
    for j in range(lines - 1):
        for step, sems in directions:

            @pl.when(jnp.logical_and(on_line(z + step), on_line(z - step * j)))
            def _():
                hop(step, sems, j).wait_send()

    depth = f_ref.shape[1]
    per_depth = depth // rows
    total = jnp.zeros((window, width), jnp.float32)
    for m in range(heads):
        total = total + jnp.dot(
            fbuf[m],
            wbuf[m * per_depth : (m + 1) * per_depth].reshape(depth, width),
            preferred_element_type=jnp.float32,
        )
    values = total.astype(jnp.bfloat16)
    numer = from_state + jnp.dot(combined_low, values, preferred_element_type=jnp.float32)
    hidden_ref[...] = (numer / denominator * live).astype(jnp.bfloat16)
    state_ref[...] = kept * start_state.astype(jnp.float32) + lax.dot_general(
        key_scaled, values, (((0,), (0,)), ((), ())), preferred_element_type=jnp.float32
    )
    grad = part[me] + yrecv[z].astype(jnp.float32)
    for k, copy in enumerate(z_copies):
        copy.wait()
        grad = grad + zrecv[lax.rem(z + lines - k - 1, lines)].astype(jnp.float32)
    grad_ref[...] = grad


def in_one_kernel(
    stream_map,
    lengths,
    features,
    query_rows,
    key_rows,
    log_forget,
    in_gate,
    value_weight,
    state,
    norm_state,
    cotangent,
):
    slots, heads = lax.axis_size("dp"), lax.axis_size("mp")
    window, width = query_rows.shape[1:]
    depth = features.shape[2]
    rows = value_weight.shape[0]
    row_part = width // slots
    lines = slots // 2
    low = jnp.bfloat16
    sems = pltpu.SemaphoreType.DMA
    vmem = pl.BlockSpec(memory_space=pltpu.VMEM)
    smem = pl.BlockSpec(memory_space=pltpu.SMEM)
    hidden, new_state, new_norm, grad = pl.pallas_call(
        functools.partial(window_kernel, slots, heads),
        out_shape=(
            jax.ShapeDtypeStruct((window, width), low),
            jax.ShapeDtypeStruct((width, width), jnp.float32),
            jax.ShapeDtypeStruct((1, width), jnp.float32),
            jax.ShapeDtypeStruct((rows, width), jnp.float32),
        ),
        in_specs=[smem, smem] + [pl.BlockSpec(memory_space=pltpu.HBM)] * 9,
        out_specs=(vmem, vmem, vmem, vmem),
        scratch_shapes=[
            pltpu.VMEM((window, width), low),
            pltpu.VMEM((window, width), low),
            pltpu.VMEM((1, window), jnp.float32),
            pltpu.VMEM((1, window), jnp.float32),
            pltpu.VMEM((slots, row_part, width), jnp.float32),
            pltpu.VMEM((window, width), low),
            pltpu.VMEM((heads, window, depth), low),
            pltpu.VMEM((slots, rows, width), low),
            pltpu.VMEM((slots, 1, width), jnp.float32),
            pltpu.VMEM((slots, row_part, width), low),
            pltpu.VMEM((slots, row_part, width), low),
            pltpu.VMEM((slots, row_part, width), low),
            pltpu.VMEM((slots, row_part, width), low),
            pltpu.VMEM((slots, rows, width), jnp.float32),
            pltpu.VMEM((slots, rows, width), low),
            pltpu.VMEM((lines, rows, width), low),
            pltpu.VMEM((lines, rows, width), low),
            pltpu.VMEM((lines, rows, width), low),
            sems((2, heads)),
            sems((2, slots)),
            sems((2, slots)),
            sems((2, slots)),
            sems((2, lines)),
            sems((2, lines)),
            sems((2, lines)),
            sems((9,)),
            sems((2, lines)),
            sems((2, lines)),
        ],
        compiler_params=pltpu.CompilerParams(
            collective_id=0, has_side_effects=True, vmem_limit_bytes=60 * 1024 * 1024
        ),
    )(
        stream_map,
        lengths,
        features[0],
        query_rows[0],
        key_rows[0],
        log_forget.reshape(1, window),
        in_gate.reshape(1, window),
        value_weight,
        state[0, 0].reshape(slots, row_part, width),
        norm_state[0],
        cotangent[0],
    )
    return (hidden[None], new_state[None, None], new_norm[None], grad)


def on_device(*args):
    slots, heads = lax.axis_size("dp"), lax.axis_size("mp")
    depth, rows, width = args[2].shape[2], args[7].shape[0], args[8].shape[-1]
    whole_tiles = slots % 2 == 0 and width % (16 * slots) == 0 and rows % 128 == 0
    if whole_tiles and depth % rows == 0 and depth * heads == rows * slots:
        return in_one_kernel(*args)
    return with_collectives(*args)


def solution(mesh):
    return jax.shard_map(
        on_device,
        mesh=mesh,
        in_specs=(
            P(),
            P("dp"),
            P("dp", None, "mp"),
            P("dp", None, "mp"),
            P("dp", None, "mp"),
            P("dp", None, "mp"),
            P("dp", None, "mp"),
            P("dp", "mp"),
            P("dp", "mp", None, None),
            P("dp", "mp", None),
            P("dp", None, "mp"),
        ),
        out_specs=(
            P("dp", None, "mp"),
            P("dp", "mp", None, None),
            P("dp", "mp", None),
            P("dp", "mp"),
        ),
        check_vma=False,
    )
```

```python
import functools

import jax
import jax.numpy as jnp
from jax import lax
from jax.experimental import pallas as pl
from jax.experimental.pallas import tpu as pltpu
from jax.sharding import PartitionSpec as P


def migrate(stream_map, state, norm_state):
    slot_count = lax.axis_size("dp")
    head_width = state.shape[-1]
    row_part = head_width // slot_count
    blocks = state[0, 0].astype(jnp.bfloat16).reshape(slot_count, row_part, head_width)
    spread = lax.all_to_all(blocks, "dp", split_axis=0, concat_axis=0, tiled=True)
    norms = lax.all_gather(norm_state[0, 0], "dp", axis=0, tiled=False)
    chosen = jnp.arange(slot_count, dtype=jnp.int32)[:, None] == stream_map[None, :]
    picked = jnp.einsum(
        "ps,src->prc",
        chosen.astype(jnp.bfloat16),
        spread,
        preferred_element_type=jnp.float32,
    ).astype(jnp.bfloat16)
    returned = lax.all_to_all(picked, "dp", split_axis=0, concat_axis=0, tiled=True)
    mine = lax.axis_index("dp") == stream_map
    start_norm = jnp.sum(jnp.where(mine[:, None], norms, 0.0), axis=0)
    return (returned.reshape(head_width, head_width), start_norm)


def window_terms(feature_all, value_weight, queries, key_vectors, forget_logs, gate_logs, length):
    window = queries.shape[0]
    head_width = queries.shape[1]
    values = jnp.dot(
        feature_all,
        lax.all_gather(value_weight, "dp", axis=0, tiled=True),
        preferred_element_type=jnp.float32,
    ).astype(jnp.bfloat16)
    position = jnp.arange(window, dtype=jnp.int32)
    live_mask = (position < length).astype(jnp.float32)
    weights_in = jnp.exp(gate_logs) * live_mask
    causal = position[:, None] >= position[None, :]
    decays = jnp.sum(jnp.where(causal, (forget_logs * live_mask)[None, :], 0.0), axis=1)
    gap_logs = jnp.where(causal, decays[:, None] - decays[None, :], -1e30)
    mixing = jnp.exp(gap_logs) * weights_in[None, :]
    scores = lax.dot_general(
        queries, key_vectors, (((1,), (1,)), ((), ())), preferred_element_type=jnp.float32
    ) * head_width ** (-0.5)
    combined = mixing * scores
    combined_low = combined.astype(jnp.bfloat16)
    local_numer = jnp.dot(combined_low, values, preferred_element_type=jnp.float32)
    local_inner = jnp.sum(combined, axis=1)
    return (values, live_mask, decays, weights_in, combined_low, local_numer, local_inner)


def with_collectives(
    stream_map,
    lengths,
    features,
    query_rows,
    key_rows,
    log_forget,
    in_gate,
    value_weight,
    state,
    norm_state,
    cotangent,
):
    feature_all = lax.all_gather(features, "mp", axis=2, tiled=True)[0]
    queries = query_rows[0]
    key_vectors = key_rows[0]
    head_width = queries.shape[1]
    window = queries.shape[0]
    start_state, start_norm = migrate(stream_map, state, norm_state)
    terms = window_terms(
        feature_all,
        value_weight,
        queries,
        key_vectors,
        log_forget[0, :, 0],
        in_gate[0, :, 0],
        lengths[0],
    )
    values, live_mask, decays, weights_in, combined_low, local_numer, local_inner = terms
    carried = jnp.exp(decays)
    query_wide = queries.astype(jnp.float32)
    from_state = jnp.dot(queries, start_state, preferred_element_type=jnp.float32)
    numer = carried[:, None] * from_state + local_numer
    inner_dot = (
        carried * jnp.sum(query_wide * start_norm[None, :], axis=1) + local_inner
    )
    denominator = jnp.maximum(jnp.abs(inner_dot), 1.0)
    hidden = (numer / denominator[:, None] * live_mask[:, None]).astype(jnp.bfloat16)
    final_decay = decays[window - 1]
    tail_weight = jnp.exp(final_decay - decays) * weights_in * head_width ** (-0.5)
    key_scaled = (key_vectors.astype(jnp.float32) * tail_weight[:, None]).astype(jnp.bfloat16)
    new_state = jnp.exp(final_decay) * start_state.astype(jnp.float32) + lax.dot_general(
        key_scaled, values, (((0,), (0,)), ((), ())), preferred_element_type=jnp.float32
    )
    new_norm = jnp.exp(final_decay) * start_norm + jnp.sum(
        tail_weight[:, None] * key_vectors.astype(jnp.float32), axis=0
    )
    scaled = (cotangent[0].astype(jnp.float32) * (live_mask / denominator)[:, None]).astype(
        jnp.bfloat16
    )
    value_grad = lax.dot_general(
        combined_low, scaled, (((0,), (0,)), ((), ())), preferred_element_type=jnp.float32
    ).astype(jnp.bfloat16)
    weight_grad = lax.psum_scatter(
        lax.dot_general(
            feature_all, value_grad, (((0,), (0,)), ((), ())), preferred_element_type=jnp.float32
        ),
        "dp",
        scatter_dimension=0,
        tiled=True,
    )
    return (hidden[None], new_state[None, None], new_norm[None, None], weight_grad)


def remote(src, dst, send_sem, recv_sem, peer):
    return pltpu.make_async_remote_copy(
        src_ref=src,
        dst_ref=dst,
        send_sem=send_sem,
        recv_sem=recv_sem,
        device_id=peer,
        device_id_type=pl.DeviceIdType.MESH,
    )


def window_kernel(
    slots,
    heads,
    map_ref,
    length_ref,
    f_ref,
    q_hbm,
    k_hbm,
    forget_hbm,
    gate_hbm,
    w_ref,
    s_hbm,
    n_ref,
    cot_hbm,
    hidden_ref,
    state_ref,
    norm_ref,
    grad_ref,
    q_ref,
    k_ref,
    forget_ref,
    gate_ref,
    s_ref,
    cot_ref,
    fbuf,
    wbuf,
    nbuf,
    sblk,
    s1,
    picked,
    s2,
    part,
    psend,
    yrecv,
    zsend,
    zrecv,
    f_sems,
    n_sems,
    s1_sems,
    s2_sems,
    up_sems,
    down_sems,
    wy_sems,
    local_sems,
    y_sems,
    z_sems,
):
    lines = slots // 2
    me = lax.axis_index("dp")
    head = lax.axis_index("mp")
    z, y = me // 2, lax.rem(me, 2)
    other = 1 - y
    pair = {"dp": z * 2 + other}

    def ahead(k):
        return lax.rem(me + k, slots)

    def line_ahead(k):
        return lax.rem(z + k, lines)

    moves = (
        (s_hbm, s_ref),
        (q_hbm, q_ref),
        (k_hbm, k_ref),
        (forget_hbm, forget_ref),
        (gate_hbm, gate_ref),
        (cot_hbm, cot_ref),
        (f_ref, fbuf.at[head]),
        (w_ref, wbuf.at[me]),
        (n_ref, nbuf.at[me]),
    )
    fetches = [
        pltpu.make_async_copy(src, dst, local_sems.at[i]) for i, (src, dst) in enumerate(moves)
    ]
    for fetch in fetches:
        fetch.start()

    barrier = pltpu.get_barrier_semaphore()
    for k in range(1, slots):
        pl.semaphore_signal(
            barrier, inc=1, device_id={"dp": ahead(k)}, device_id_type=pl.DeviceIdType.MESH
        )
    for k in range(1, heads):
        pl.semaphore_signal(
            barrier,
            inc=1,
            device_id={"mp": lax.rem(head + k, heads)},
            device_id_type=pl.DeviceIdType.MESH,
        )
    pl.semaphore_wait(barrier, slots + heads - 2)

    norm_copies = [
        remote(n_ref, nbuf.at[me], n_sems.at[0, k], n_sems.at[1, k], {"dp": ahead(k)})
        for k in range(1, slots)
    ]
    feature_copies = [
        remote(
            f_ref,
            fbuf.at[head],
            f_sems.at[0, k],
            f_sems.at[1, k],
            {"mp": lax.rem(head + k, heads)},
        )
        for k in range(1, heads)
    ]
    for copy in norm_copies + feature_copies:
        copy.start()
    fetches[0].wait()
    sblk[...] = s_ref[...].astype(jnp.bfloat16)
    spread_copies = [
        remote(
            sblk.at[ahead(k)], s1.at[me], s1_sems.at[0, k], s1_sems.at[1, k], {"dp": ahead(k)}
        )
        for k in range(1, slots)
    ]
    for copy in spread_copies:
        copy.start()
    def on_line(i):
        return jnp.logical_and(i >= 0, i < lines)

    def hop(step, sems, j):
        slot = (z - step * j) * 2 + y
        to = {"dp": (z + step) * 2 + y}
        source = w_ref if j == 0 else wbuf.at[slot]
        return remote(source, wbuf.at[slot], sems.at[0, j], sems.at[1, j], to)

    def arrival(step, sems, j):
        slot = (z - step * (j + 1)) * 2 + y
        to = {"dp": (z - step) * 2 + y}
        return remote(wbuf.at[slot], wbuf.at[slot], sems.at[0, j], sems.at[1, j], to)

    def hand_over(line, own=False):
        slot = line * 2 + y
        source = w_ref if own else wbuf.at[slot]
        return remote(source, wbuf.at[slot], wy_sems.at[0, line], wy_sems.at[1, line], pair)

    directions = ((1, up_sems), (-1, down_sems))

    def pass_on(j):
        for step, sems in directions:

            @pl.when(on_line(z - step * (j + 1)))
            def _():
                arrival(step, sems, j).wait_recv()
                if j + 2 < lines:

                    @pl.when(on_line(z + step))
                    def _():
                        hop(step, sems, j + 1).start()

                hand_over(z - step * (j + 1)).start()

    for step, sems in directions:

        @pl.when(on_line(z + step))
        def _():
            hop(step, sems, 0).start()

    hand_over(z, True).start()

    s1[me] = sblk[me]
    for fetch in fetches[1:6]:
        fetch.wait()

    window, width = q_ref.shape
    length = length_ref[0]
    row = lax.broadcasted_iota(jnp.int32, (window, window), 0)
    column = lax.broadcasted_iota(jnp.int32, (window, window), 1)
    causal = row >= column
    diagonal = row == column
    live = (lax.broadcasted_iota(jnp.int32, (window, 1), 0) < length).astype(jnp.float32)
    live_row = (lax.broadcasted_iota(jnp.int32, (1, window), 1) < length).astype(jnp.float32)

    weights_row = jnp.exp(gate_ref[...]) * live_row
    weights_in = jnp.sum(jnp.where(diagonal, weights_row, 0.0), axis=1, keepdims=True)
    decays = jnp.sum(
        jnp.where(causal, forget_ref[...] * live_row, 0.0), axis=1, keepdims=True
    )
    decays_row = jnp.sum(jnp.where(diagonal, decays, 0.0), axis=0, keepdims=True)
    mixing = jnp.exp(jnp.where(causal, decays - decays_row, -1e30)) * weights_row
    scale = width**-0.5
    scores = lax.dot_general(
        q_ref[...], k_ref[...], (((1,), (1,)), ((), ())), preferred_element_type=jnp.float32
    )
    combined = mixing * (scores * scale)
    combined_low = combined.astype(jnp.bfloat16)
    carried = jnp.exp(decays)
    final_decay = decays[window - 1 : window, :]
    kept = jnp.exp(final_decay)
    tail = jnp.exp(final_decay - decays) * weights_in * scale
    key_wide = k_ref[...].astype(jnp.float32) * tail
    key_scaled = key_wide.astype(jnp.bfloat16)

    def source_of(p):
        found = jnp.int32(0)
        for s in range(slots):
            found = jnp.where(map_ref[s] == p, jnp.int32(s), found)
        return found

    fetches[8].wait()
    for copy in norm_copies:
        copy.wait()
    start_norm = nbuf[source_of(me)]
    norm_ref[...] = kept * start_norm + jnp.sum(key_wide, axis=0, keepdims=True)
    inner = carried * jnp.sum(
        q_ref[...].astype(jnp.float32) * start_norm, axis=1, keepdims=True
    ) + jnp.sum(combined, axis=1, keepdims=True)
    denominator = jnp.maximum(jnp.abs(inner), 1.0)
    scaled = (cot_ref[...].astype(jnp.float32) * (live / denominator)).astype(jnp.bfloat16)
    value_grad = lax.dot_general(
        combined_low, scaled, (((0,), (0,)), ((), ())), preferred_element_type=jnp.float32
    ).astype(jnp.bfloat16)

    pass_on(0)
    for copy in spread_copies:
        copy.wait()
    for p in range(slots):
        picked[p] = s1[source_of(p)]
    return_copies = [
        remote(
            picked.at[ahead(k)], s2.at[me], s2_sems.at[0, k], s2_sems.at[1, k], {"dp": ahead(k)}
        )
        for k in range(1, slots)
    ]
    for copy in return_copies:
        copy.start()
    s2[me] = picked[me]

    fetches[6].wait()
    for copy in feature_copies:
        copy.wait()
    rows = grad_ref.shape[0]
    per_head = f_ref.shape[1] // rows

    def exchange(line):
        return remote(
            psend.at[line * 2 + other],
            yrecv.at[line],
            y_sems.at[0, line],
            y_sems.at[1, line],
            pair,
        )

    for r in range(slots):
        lower = (r % per_head) * rows
        block = lax.dot_general(
            fbuf[r // per_head, :, lower : lower + rows],
            value_grad,
            (((0,), (0,)), ((), ())),
            preferred_element_type=jnp.float32,
        )
        part[r] = block
        psend[r] = block.astype(jnp.bfloat16)

        @pl.when(other == r % 2)
        def _():
            exchange(r // 2).start()

    pass_on(1)
    z_copies = []
    for k in range(1, lines):
        to = line_ahead(k)
        exchange(to).wait()
        zsend[to] = (part[to * 2 + y] + yrecv[to].astype(jnp.float32)).astype(jnp.bfloat16)
        out = remote(
            zsend.at[to], zrecv.at[z], z_sems.at[0, k], z_sems.at[1, k], {"dp": to * 2 + y}
        )
        out.start()
        z_copies.append(out)
        if 1 < k + 1 < lines - 1:
            pass_on(k + 1)
    exchange(z).wait()

    for copy in return_copies:
        copy.wait()
    start_state = s2[...].reshape(width, width)
    from_state = carried * jnp.dot(
        q_ref[...], start_state, preferred_element_type=jnp.float32
    )
    fetches[7].wait()
    for line in range(lines):
        handed = remote(
            w_ref,
            wbuf.at[line * 2 + other],
            wy_sems.at[0, line],
            wy_sems.at[1, line],
            pair,
        )
        handed.wait()
    for j in range(lines - 1):
        for step, sems in directions:

            @pl.when(jnp.logical_and(on_line(z + step), on_line(z - step * j)))
            def _():
                hop(step, sems, j).wait_send()

    depth = f_ref.shape[1]
    per_depth = depth // rows
    total = jnp.zeros((window, width), jnp.float32)
    for m in range(heads):
        total = total + jnp.dot(
            fbuf[m],
            wbuf[m * per_depth : (m + 1) * per_depth].reshape(depth, width),
            preferred_element_type=jnp.float32,
        )
    values = total.astype(jnp.bfloat16)
    numer = from_state + jnp.dot(combined_low, values, preferred_element_type=jnp.float32)
    hidden_ref[...] = (numer / denominator * live).astype(jnp.bfloat16)
    state_ref[...] = kept * start_state.astype(jnp.float32) + lax.dot_general(
        key_scaled, values, (((0,), (0,)), ((), ())), preferred_element_type=jnp.float32
    )
    grad = part[me] + yrecv[z].astype(jnp.float32)
    for k, copy in enumerate(z_copies):
        copy.wait()
        grad = grad + zrecv[lax.rem(z + lines - k - 1, lines)].astype(jnp.float32)
    grad_ref[...] = grad


def in_one_kernel(
    stream_map,
    lengths,
    features,
    query_rows,
    key_rows,
    log_forget,
    in_gate,
    value_weight,
    state,
    norm_state,
    cotangent,
):
    slots, heads = lax.axis_size("dp"), lax.axis_size("mp")
    window, width = query_rows.shape[1:]
    depth = features.shape[2]
    rows = value_weight.shape[0]
    row_part = width // slots
    lines = slots // 2
    low = jnp.bfloat16
    sems = pltpu.SemaphoreType.DMA
    vmem = pl.BlockSpec(memory_space=pltpu.VMEM)
    smem = pl.BlockSpec(memory_space=pltpu.SMEM)
    hidden, new_state, new_norm, grad = pl.pallas_call(
        functools.partial(window_kernel, slots, heads),
        out_shape=(
            jax.ShapeDtypeStruct((window, width), low),
            jax.ShapeDtypeStruct((width, width), jnp.float32),
            jax.ShapeDtypeStruct((1, width), jnp.float32),
            jax.ShapeDtypeStruct((rows, width), jnp.float32),
        ),
        in_specs=[smem, smem] + [pl.BlockSpec(memory_space=pltpu.HBM)] * 9,
        out_specs=(vmem, vmem, vmem, vmem),
        scratch_shapes=[
            pltpu.VMEM((window, width), low),
            pltpu.VMEM((window, width), low),
            pltpu.VMEM((1, window), jnp.float32),
            pltpu.VMEM((1, window), jnp.float32),
            pltpu.VMEM((slots, row_part, width), jnp.float32),
            pltpu.VMEM((window, width), low),
            pltpu.VMEM((heads, window, depth), low),
            pltpu.VMEM((slots, rows, width), low),
            pltpu.VMEM((slots, 1, width), jnp.float32),
            pltpu.VMEM((slots, row_part, width), low),
            pltpu.VMEM((slots, row_part, width), low),
            pltpu.VMEM((slots, row_part, width), low),
            pltpu.VMEM((slots, row_part, width), low),
            pltpu.VMEM((slots, rows, width), jnp.float32),
            pltpu.VMEM((slots, rows, width), low),
            pltpu.VMEM((lines, rows, width), low),
            pltpu.VMEM((lines, rows, width), low),
            pltpu.VMEM((lines, rows, width), low),
            sems((2, heads)),
            sems((2, slots)),
            sems((2, slots)),
            sems((2, slots)),
            sems((2, lines)),
            sems((2, lines)),
            sems((2, lines)),
            sems((9,)),
            sems((2, lines)),
            sems((2, lines)),
        ],
        compiler_params=pltpu.CompilerParams(
            collective_id=0, has_side_effects=True, vmem_limit_bytes=60 * 1024 * 1024
        ),
    )(
        stream_map,
        lengths,
        features[0],
        query_rows[0],
        key_rows[0],
        log_forget.reshape(1, window),
        in_gate.reshape(1, window),
        value_weight,
        state[0, 0].reshape(slots, row_part, width),
        norm_state[0],
        cotangent[0],
    )
    return (hidden[None], new_state[None, None], new_norm[None], grad)


def on_device(*args):
    slots, heads = lax.axis_size("dp"), lax.axis_size("mp")
    depth, rows, width = args[2].shape[2], args[7].shape[0], args[8].shape[-1]
    whole_tiles = slots % 2 == 0 and width % (16 * slots) == 0 and rows % 128 == 0
    if whole_tiles and depth % rows == 0 and depth * heads == rows * slots:
        return in_one_kernel(*args)
    return with_collectives(*args)


def solution(mesh):
    return jax.shard_map(
        on_device,
        mesh=mesh,
        in_specs=(
            P(),
            P("dp"),
            P("dp", None, "mp"),
            P("dp", None, "mp"),
            P("dp", None, "mp"),
            P("dp", None, "mp"),
            P("dp", None, "mp"),
            P("dp", "mp"),
            P("dp", "mp", None, None),
            P("dp", "mp", None),
            P("dp", None, "mp"),
        ),
        out_specs=(
            P("dp", None, "mp"),
            P("dp", "mp", None, None),
            P("dp", "mp", None),
            P("dp", "mp"),
        ),
        check_vma=False,
    )
```
